256 devices in a mesh: row: 32 (over x, z_lo, core), col: 8 (over z_hi, y).
Axes of the slice: x: 4, y: 4, z: 8 (z_hi: 2, z_lo: 4; z = z_hi * 4 + z_lo), core: 2. Of those that a mesh axis runs over, the one named last changes fastest.
Arguments:
- inverse_anc: float32 [8192, 8192], P('row', 'col'), as said below
- lower_panel: float32 [8192, 2048], P('row', 'col'), may hold values from -0.5 to 0.5
- structure: int32 [8, 16], P('col'), may hold values from 0 to 31, as said below
- diag_inverse: float32 [2048, 256], P('col'), may hold values from -6 to 6
Outputs:
- inverse_panel: float32 [8192, 2048], P('row', 'col')
- diagonal_block: float32 [2048, 256], P('col')
The draws below stay inside these ranges and needn't reach their ends.
Inputs may be any that keep to these rules, and one draw needn't show every extreme that they name: inverse_anc is exactly symmetric. `structure`: each row lists 16 different ancestor block numbers in increasing order; each index of col holds exactly one row (one lower supernode).
All inputs are finite; a program needn't handle non-finite values.
Results may differ from the reference program's by a relative error of at most 0.000075.
Values sent between devices are 32-bit elements; how exact they have to be, the bound alone decides.
A program may use at most 64 MiB of HBM per device.

```python
import math
import jax
import jax.numpy as jnp
from jax import lax

B = 256
ANC = 32
STR = 16
SN_DEV = 1
NS = 8
ORDER = 8192


def draw_inverse_anc(key, part):
    matrix_order = ANC * B
    key_first = jax.random.fold_in(jax.random.fold_in(key, 11), 0)
    normal_base = jax.random.normal(key_first, (matrix_order, matrix_order), jnp.float32)
    symmetric = (normal_base + normal_base.T) / math.sqrt(2.0 * matrix_order)
    return symmetric + jnp.eye(matrix_order, dtype=jnp.float32)


def draw_structure(key, part):
    groups = NS // SN_DEV
    rounds = (SN_DEV * STR + ANC - 1) // ANC
    positions = jnp.arange(ANC, dtype=jnp.int32)
    scores = jax.random.randint(jax.random.fold_in(key, 7), (groups, rounds, ANC), 0, 1048576, dtype=jnp.int32)
    scores = scores * ANC + positions[None, None, :]
    orders = jnp.argsort(scores, axis=2).astype(jnp.int32)
    supernodes = jnp.arange(NS, dtype=jnp.int32)
    group_ids = supernodes // SN_DEV
    slot_ids = supernodes % SN_DEV
    round_ids = slot_ids * STR // ANC
    offsets = slot_ids * STR % ANC
    columns = offsets[:, None] + jnp.arange(STR, dtype=jnp.int32)[None, :]
    picked = orders[group_ids[:, None], round_ids[:, None], columns]
    return jnp.sort(picked, axis=1).astype(jnp.int32)


def level_of(stream_key, dims, shards, low, high):
    factor_of, own = 1.0, jax.random.fold_in(stream_key, 6)
    for axis_at, parts in shards:
        heights = jnp.exp(jax.random.uniform(jax.random.fold_in(own, axis_at), (parts,), jnp.float32, low / len(shards), high / len(shards)))
        factor_of = factor_of * jnp.repeat(heights, dims[axis_at] // parts).reshape([-1 if axis == axis_at else 1 for axis in range(len(dims))])
    return factor_of


def bell_draw(stream_key, shape, spread, bound, shards=(), kind=jnp.bfloat16):
    gain = level_of(stream_key, shape, shards, -0.22, 0.18) if shards else 1.0
    entries = jax.random.normal(stream_key, shape, jnp.float32) * spread * gain
    return jnp.minimum(jnp.maximum(entries, -bound), bound).astype(kind)


def setup_inputs(seed: int = 0) -> dict:
    keys = jax.random.split(jax.random.key(seed), 5)
    return {
        "inverse_anc": draw_inverse_anc(jax.random.fold_in(keys[4], 71), 0),
        "lower_panel": bell_draw(keys[1], (ORDER, NS * B), 0.0625, 0.5, ((0, 32), (1, 8)), jnp.float32),
        "structure": draw_structure(jax.random.fold_in(keys[4], 71), 0),
        "diag_inverse": bell_draw(keys[3], (NS * B, B), 1.0, 6.0, ((0, 8),), jnp.float32),
    }


def keep_rows(structure, first_row, row_count, sn_width):
    block_ids = (first_row + jnp.arange(row_count, dtype=jnp.int32)) // sn_width
    listed = jnp.any(structure[None, :, :] == block_ids[:, None, None], axis=2)
    return jnp.repeat(listed, sn_width, axis=1)


def reference(inverse_anc, lower_panel, structure, diag_inverse):
    matrix_order = inverse_anc.shape[0]
    keep_mask = keep_rows(structure, jnp.int32(0), matrix_order, B)
    masked = jnp.where(keep_mask, lower_panel, jnp.float32(0.0))
    product = jnp.dot(inverse_anc, masked, precision=lax.Precision.HIGHEST, preferred_element_type=jnp.float32)
    panel = jnp.where(keep_mask, -product, jnp.float32(0.0))
    lower_blocks = masked.reshape(matrix_order, NS, B)
    panel_blocks = panel.reshape(matrix_order, NS, B)
    terms = jnp.einsum("ika,ikb->kab", lower_blocks, panel_blocks, precision=lax.Precision.HIGHEST)
    return panel, diag_inverse - terms.reshape(NS * B, B)
```

```python
import functools

import jax
import jax.numpy as jnp
from jax import lax
from jax.experimental import pallas as pl
from jax.experimental.pallas import tpu as pltpu
from jax.sharding import PartitionSpec as P

MESH = pl.DeviceIdType.MESH
Q = 2
W = 128
B = 256


def device(x, zl, core, zh, y):
    return ((x * 4 + zl) * 2 + core, zh * 4 + y)


def slot_of(zl, same):
    high = zl // 2
    return same * zl + (1 - same) * (high * (3 - zl) + (1 - high) * (2 + zl))


def split(value):
    high = value.astype(jnp.bfloat16)
    return high, (value - high.astype(jnp.float32)).astype(jnp.bfloat16)


def dot3(a_high, a_low, b_high, b_low):
    dot = functools.partial(jnp.dot, preferred_element_type=jnp.float32)
    return dot(a_high, b_high) + (dot(a_high, b_low) + dot(a_low, b_high))


def kernel(
    a_ref, m_ref, st_ref, dinv_ref, p_ref, d_ref,
    a_own, a_other, a_hi, a_lo, m_in, m_own, mt_hi, mt_lo, m_all, m_hi, m_lo,
    part, c1, c2, nf, t_buf, t_in, t_out,
    load_sem, a_sem, home_s, home_r, z_s, z_r, x_s, x_r, f_s, f_r,
    c1_s, c1_r, c2_s, c2_r, n_s, n_r, fz_s, fz_r, t_s, t_r, o_s, o_r,
):
    row = lax.axis_index("row")
    col = lax.axis_index("col")
    x, zl, core = row // 8, (row // 2) % 4, row % 2
    zh, y = col // 4, col % 4

    load_m = pltpu.make_async_copy(m_ref, m_in, load_sem.at[0])
    load_m.start()
    load_a = pltpu.make_async_copy(a_ref, a_own, load_sem.at[1])
    load_a.start()

    b = zl % 2
    to_zh, to_y = x // 2, (x % 2) * 2 + zl // 2
    same = 1 - (zh - to_zh) * (zh - to_zh)
    to_x = (y + x) % 4
    to_zl = same * (2 * b + core) + (1 - same) * ((1 - b) * (3 - core) + b * core)
    off = (
        (to_x - x) * (to_x - x) + (to_zl - zl) * (to_zl - zl) + (zh - core) * (zh - core)
        + (to_zh - zh) * (to_zh - zh) + (to_y - y) * (to_y - y)
    )
    home = device(to_x, to_zl, zh, to_zh, to_y)
    from_x = 2 * zh + y // 2
    same_half = 1 - (core - zh) * (core - zh)
    j4 = slot_of(zl, same_half)
    from_y = (x - from_x + 4) % 4
    source = device(from_x, 2 * (y % 2) + j4 // 2, j4 % 2, core, from_y)

    far = (core - zh) * (core - zh)
    right_y, left_y = (y + 1) % 4, (y + 3) % 4

    barrier = pltpu.get_barrier_semaphore()

    def greet(d, carry):
        pl.semaphore_signal(barrier, inc=1, device_id=((row + d) % 32, col), device_id_type=MESH)
        return carry

    lax.fori_loop(1, 32, greet, 0)
    pl.semaphore_signal(barrier, inc=1, device_id=(row, zh * 4 + right_y), device_id_type=MESH)
    pl.semaphore_signal(barrier, inc=1, device_id=(row, zh * 4 + left_y), device_id_type=MESH)
    pl.semaphore_signal(barrier, inc=1, device_id=device(x, zl, zh, 1 - zh, y), device_id_type=MESH)

    @pl.when(off > 0)
    def _():
        pl.semaphore_signal(barrier, inc=1, device_id=source, device_id_type=MESH)

    listed = st_ref[0, 0] == row
    for s in range(1, 16):
        listed = listed | (st_ref[0, s] == row)
    keep = jnp.where(listed, 1, 0)
    load_m.wait()
    masked = jnp.where(jnp.broadcast_to(keep, (B, B)) > 0, m_in[...], 0.0)
    for q in range(Q):
        m_own[q] = masked[:, q * W:(q + 1) * W]

    pl.semaphore_wait(barrier, 33 + 2 * far + jnp.minimum(off, 1))

    def remote(src, dst, send, recv, target):
        return pltpu.make_async_remote_copy(
            src_ref=src, dst_ref=dst, send_sem=send, recv_sem=recv,
            device_id=target, device_id_type=MESH,
        )

    own_slot = 2 * b + core
    sends = []
    for q in range(Q):
        @pl.when(off > 0)
        def _(q=q):
            remote(m_own.at[q], m_all.at[q, own_slot, y], home_s.at[q], home_r.at[q], home).start()

        @pl.when(off == 0)
        def _(q=q):
            pltpu.make_async_copy(m_own.at[q], m_all.at[q, own_slot, y], home_r.at[q]).start()

    a_copy = remote(a_ref, a_other, a_sem.at[0], a_sem.at[1], device(x, zl, 1 - core, zh, y))
    a_copy.start()

    mt_hi[...], mt_lo[...] = split(masked.T)

    load_a.wait()
    hi, lo = split(a_own[...])
    a_hi[core], a_lo[core] = hi, lo

    def unit(q, h, at_x):
        return m_all.at[q, slot_of(h, same_half), (at_x - from_x + 8) % 4]

    def z_send(q):
        for i, d in enumerate((1, 3, 2)):
            cp = remote(unit(q, zl, x), unit(q, zl, x), z_s.at[q, i], z_r.at[q, zl],
                        device(x, (zl + d) % 4, core, zh, y))
            cp.start()
            sends.append(cp)

    def x_send(q, h):
        for i, d in enumerate((1, 3)):
            cp = remote(unit(q, h, x), unit(q, h, x), x_s.at[q, h, i], x_r.at[q, h, i],
                        device((x + d) % 4, zl, core, zh, y))
            cp.start()
            sends.append(cp)

    def x_wait(q, h, i):
        src = unit(q, h, x + (3 if i == 0 else 1))
        remote(src, src, x_s.at[q, h, i], x_r.at[q, h, i], device((x + 1) % 4, zl, core, zh, y)).wait_recv()

    def home_wait(q):
        u = unit(q, zl, x)
        pltpu.make_async_copy(u, u, home_r.at[q]).wait()

    order = (0, 1, 3, 2)

    def forward(q, h, i):
        u = unit(q, h, x + (3 if i == 0 else 1))
        cp = remote(u, u, f_s.at[q, h], f_r.at[q, h],
                    device((x + (1 if i == 0 else 3)) % 4, zl, core, zh, y))
        cp.start()
        sends.append(cp)

    def x_sends(q):
        x_send(q, zl)
        for d in order[1:]:
            h = (zl + d) % 4
            u = unit(q, h, x)
            remote(u, u, z_s.at[q, 0], z_r.at[q, h], device(x, (zl + 1) % 4, core, zh, y)).wait_recv()
            x_send(q, h)

    def forwards(q):
        for h in range(4):
            x_wait(q, h, h % 2)
            forward(q, h, h % 2)

    def gathered(q):
        for h in range(4):
            x_wait(q, h, 1 - h % 2)
        for h in range(4):
            u = unit(q, h, x + 2)
            remote(u, u, f_s.at[q, h], f_r.at[q, h], device((x + 1) % 4, zl, core, zh, y)).wait_recv()

    def multiply(q):
        for j in range(4):
            for k in range(4):
                hi, lo = split(m_all[q, j, k])
                m_hi[j * B:(j + 1) * B, k * W:(k + 1) * W] = hi
                m_lo[j * B:(j + 1) * B, k * W:(k + 1) * W] = lo
        for r in range(2):
            out = dot3(a_hi[r], a_lo[r], m_hi[...], m_lo[...])
            for k in range(4):
                part[q, k, r] = out[:, k * W:(k + 1) * W]

    def to_right(src, dst, send, recv):
        cp = remote(src, dst, send, recv, (row, zh * 4 + right_y))
        cp.start()
        sends.append(cp)

    def to_left(src, dst, send, recv):
        cp = remote(src, dst, send, recv, (row, zh * 4 + left_y))
        cp.start()
        sends.append(cp)

    def scatter_first(q):
        over = (y + 2) % 4
        to_right(part.at[q, over, 0], c1.at[q, 0], c1_s.at[q, 0], c1_r.at[q, 0])
        to_left(part.at[q, over, 1], c1.at[q, 1], c1_s.at[q, 1], c1_r.at[q, 1])
        to_right(part.at[q, right_y, 1], c2.at[q, 0, 1], c2_s.at[q, 0, 1], c2_r.at[q, 0, 1])
        to_left(part.at[q, left_y, 0], c2.at[q, 1, 0], c2_s.at[q, 1, 0], c2_r.at[q, 1, 0])

    def arrived(buf, send, recv):
        remote(buf, buf, send, recv, (row, zh * 4 + right_y)).wait_recv()

    def scatter_second(q):
        arrived(c1.at[q, 0], c1_s.at[q, 0], c1_r.at[q, 0])
        part[q, right_y, 0] = part[q, right_y, 0] + c1[q, 0]
        to_right(part.at[q, right_y, 0], c2.at[q, 0, 0], c2_s.at[q, 0, 0], c2_r.at[q, 0, 0])
        arrived(c1.at[q, 1], c1_s.at[q, 1], c1_r.at[q, 1])
        part[q, left_y, 1] = part[q, left_y, 1] + c1[q, 1]
        to_left(part.at[q, left_y, 1], c2.at[q, 1, 1], c2_s.at[q, 1, 1], c2_r.at[q, 1, 1])

    def scatter_last(q):
        for r in range(2):
            for i in range(2):
                arrived(c2.at[q, i, r], c2_s.at[q, i, r], c2_r.at[q, i, r])
        for r in range(2):
            part[q, y, r] = part[q, y, r] + (c2[q, 0, r] + c2[q, 1, r])

        @pl.when(far == 0)
        def _():
            remote(part.at[q, y, 1 - core], nf.at[q, 0], n_s.at[q], n_r.at[q],
                   device(x, zl, 1 - core, zh, y)).start()
            nf[q, 0] = part[q, y, core]

        @pl.when(far == 1)
        def _():
            for r in range(2):
                remote(part.at[q, y, r], nf.at[q, 1], fz_s.at[q, r], fz_r.at[q],
                       device(x, zl, r, 1 - zh, y)).start()

    def finish(q):
        @pl.when(far == 1)
        def _():
            arrived(nf.at[q, 0], n_s.at[q], n_r.at[q])

        arrived(nf.at[q, 1], fz_s.at[q, 0], fz_r.at[q])
        panel = jnp.where(jnp.broadcast_to(keep, (B, W)) > 0, -(nf[q, 0] + nf[q, 1]), 0.0)
        p_ref[:, q * W:(q + 1) * W] = panel
        p_hi, p_lo = split(panel)
        t_buf[:, :, q * W:(q + 1) * W] = dot3(mt_hi[...], mt_lo[...], p_hi, p_lo).reshape(32, 8, W)

    home_wait(0)
    z_send(0)
    home_wait(1)
    z_send(1)
    x_sends(0)
    a_copy.wait()
    hi, lo = split(a_other[...])
    a_hi[1 - core], a_lo[1 - core] = hi, lo
    forwards(0)
    x_sends(1)
    gathered(0)
    multiply(0)
    scatter_first(0)
    forwards(1)
    scatter_second(0)
    scatter_last(0)
    gathered(1)
    multiply(1)
    scatter_first(1)
    scatter_second(1)
    finish(0)
    scatter_last(1)
    finish(1)

    def t_copy(d):
        peer = (row + d) % 32
        return remote(t_buf.at[peer], t_in.at[row], t_s.at[d], t_r.at[0], (peer, col))

    def o_copy(d):
        peer = (row + d) % 32
        return remote(t_out.at[row], t_out.at[row], o_s.at[d], o_r.at[0], (peer, col))

    def start(copy):
        def body(d, carry):
            copy(d).start()
            return carry
        lax.fori_loop(1, 32, body, 0)

    start(t_copy)
    t_in[row] = t_buf[row]
    every = t_in.at[pl.ds(0, 31)]
    remote(every, every, t_s.at[0], t_r.at[0], ((row + 1) % 32, col)).wait_recv()
    total = jnp.sum(t_in[...], axis=0)
    first = pl.multiple_of(row * 8, 8)
    t_out[row] = dinv_ref[pl.ds(first, 8), :] - total
    start(o_copy)
    every = t_out.at[pl.ds(0, 31)]
    remote(every, every, o_s.at[0], o_r.at[0], ((row + 1) % 32, col)).wait_recv()
    d_ref[...] = t_out[...].reshape(B, B)

    for cp in sends:
        cp.wait_send()
    for q in range(Q):
        @pl.when(off > 0)
        def _(q=q):
            remote(m_own.at[q], m_all.at[q, own_slot, y], home_s.at[q], home_r.at[q], home).wait_send()

        @pl.when(far == 0)
        def _(q=q):
            remote(part.at[q, y, 1 - core], nf.at[q, 0], n_s.at[q], n_r.at[q],
                   device(x, zl, 1 - core, zh, y)).wait_send()

        @pl.when(far == 1)
        def _(q=q):
            for r in range(2):
                remote(part.at[q, y, r], nf.at[q, 1], fz_s.at[q, r], fz_r.at[q],
                       device(x, zl, r, 1 - zh, y)).wait_send()

    def left(d, carry):
        t_copy(d).wait_send()
        o_copy(d).wait_send()
        return carry

    lax.fori_loop(1, 32, left, 0)


def local(inverse_anc, lower_panel, structure, diag_inverse):
    f32, bf16 = jnp.float32, jnp.bfloat16
    dma = pltpu.SemaphoreType.DMA
    hbm = pl.BlockSpec(memory_space=pl.ANY)
    vmem = pl.BlockSpec(memory_space=pltpu.VMEM)
    return pl.pallas_call(
        kernel,
        out_shape=(jax.ShapeDtypeStruct((B, B), f32), jax.ShapeDtypeStruct((B, B), f32)),
        in_specs=[hbm, hbm, pl.BlockSpec(memory_space=pltpu.SMEM), vmem],
        out_specs=(vmem, vmem),
        scratch_shapes=[
            pltpu.VMEM((B, 4 * B), f32), pltpu.VMEM((B, 4 * B), f32),
            pltpu.VMEM((2, B, 4 * B), bf16), pltpu.VMEM((2, B, 4 * B), bf16),
            pltpu.VMEM((B, B), f32), pltpu.VMEM((Q, B, W), f32),
            pltpu.VMEM((B, B), bf16), pltpu.VMEM((B, B), bf16),
            pltpu.VMEM((Q, 4, 4, B, W), f32),
            pltpu.VMEM((4 * B, 4 * W), bf16), pltpu.VMEM((4 * B, 4 * W), bf16),
            pltpu.VMEM((Q, 4, 2, B, W), f32),
            pltpu.VMEM((Q, 2, B, W), f32), pltpu.VMEM((Q, 2, 2, B, W), f32),
            pltpu.VMEM((Q, 2, B, W), f32),
            pltpu.VMEM((32, 8, B), f32), pltpu.VMEM((32, 8, B), f32), pltpu.VMEM((32, 8, B), f32),
            dma((2,)), dma((2,)), dma((Q,)), dma((Q,)), dma((Q, 3)), dma((Q, 4)),
            dma((Q, 4, 2)), dma((Q, 4, 2)), dma((Q, 4)), dma((Q, 4)),
            dma((Q, 2)), dma((Q, 2)), dma((Q, 2, 2)), dma((Q, 2, 2)),
            dma((Q,)), dma((Q,)), dma((Q, 2)), dma((Q,)),
            dma((32,)), dma((1,)), dma((32,)), dma((1,)),
        ],
        compiler_params=pltpu.CompilerParams(
            collective_id=0, has_side_effects=True, vmem_limit_bytes=48 * 2**20
        ),
    )(inverse_anc, lower_panel, structure, diag_inverse)


def solution(mesh):
    placed = (P("row", "col"), P("row", "col"), P("col", None), P("col", None))
    return jax.shard_map(
        local,
        mesh=mesh,
        in_specs=placed,
        out_specs=(P("row", "col"), P("col", None)),
        check_vma=False,
    )
```

```python
import functools

import jax
import jax.numpy as jnp
from jax import lax
from jax.experimental import pallas as pl
from jax.experimental.pallas import tpu as pltpu
from jax.sharding import PartitionSpec as P

MESH = pl.DeviceIdType.MESH
Q = 2
W = 128
B = 256
OWN, NEXT = 0, 1


def device(x, zl, core, zh, y):
    return ((x * 4 + zl) * 2 + core, zh * 4 + y)


def differ(a, b):
    return a + b - 2 * a * b


def split(value):
    high = value.astype(jnp.bfloat16)
    return high, (value - high.astype(jnp.float32)).astype(jnp.bfloat16)


def dot3(a_high, a_low, b_high, b_low):
    dot = functools.partial(jnp.dot, preferred_element_type=jnp.float32)
    return dot(a_high, b_high) + (dot(a_high, b_low) + dot(a_low, b_high))


def kernel(
    a_ref, m_ref, st_ref, dinv_ref, p_ref, d_ref,
    a_own, a_mate, a_next, a_far, a_hi, a_lo, m_in, m_own, mt_hi, mt_lo, m_all, m_hi, m_lo,
    part, c1, c2, nf, t_buf, t_in, z_in, t_out, dinv,
    load_sem, am_sem, an_s, an_r, af_s, af_r, home_s, home_r, z_s, z_r, x_s, x_r, f_s, f_r,
    e1_s, c1_r, o_s, c2_r, n_s, n_r, ds_s, ds_r, dz_s, dz_r, dg_s, dg_r,
):
    row = lax.axis_index("row")
    col = lax.axis_index("col")
    x, zl, core = row // 8, (row // 2) % 4, row % 2
    zh, y = col // 4, col % 4
    t, s = zl // 2, zl % 2

    load_m = pltpu.make_async_copy(m_ref, m_in, load_sem.at[0])
    load_m.start()
    load_a = pltpu.make_async_copy(a_ref, a_own, load_sem.at[1])
    load_a.start()
    load_d = pltpu.make_async_copy(dinv_ref, dinv, load_sem.at[2])
    load_d.start()

    to_zh, to_y = x // 2, (x % 2) * 2 + t
    turn = differ(zh, to_zh) * differ(t, zh)
    to_x = (2 * core + y // 2 + x) % 4
    to_zl = 2 * differ(s, turn) + zh
    home = device(to_x, to_zl, y % 2, to_zh, to_y)
    off = (
        (to_x - x) * (to_x - x) + (to_zl - zl) * (to_zl - zl) + (y % 2 - core) * (y % 2 - core)
        + (to_zh - zh) * (to_zh - zh) + (to_y - y) * (to_y - y)
    )
    from_x = 2 * zh + y // 2
    turned = differ(s, zh) * differ(y % 2, s)

    def block_of(at_x, at_t):
        m = (at_x - from_x + 8) % 4
        return 2 * differ(at_t, turned) + m // 2, m % 2

    def unit(q, at_x, at_t):
        j, i = block_of(at_x, at_t)
        return m_all.at[q, j, i]

    j_here, i_here = block_of(x, t)
    source = device(from_x, 2 * (y % 2) + j_here // 2, j_here % 2, s, 2 * i_here + core)

    even = 1 - differ(core, y % 2)
    apart = differ(zh, s)
    right_y, left_y = (y + 1) % 4, (y + 3) % 4
    right, left = (row, zh * 4 + right_y), (row, zh * 4 + left_y)
    mate = device(x, zl, 1 - core, zh, y)
    nextz = device(x, 2 * t + 1 - s, core, zh, y)
    me = x * 2 + core

    barrier = pltpu.get_barrier_semaphore()

    def greet(target):
        pl.semaphore_signal(barrier, inc=1, device_id=target, device_id_type=MESH)

    def peer_x(e):
        return device(e // 2, zl, e % 2, zh, y)

    for d in range(1, 8):
        greet(peer_x((me + d) % 8))
    for d in range(1, 4):
        greet(device(x, (zl + d) % 4, core, zh, y))
    greet(right)
    greet(left)
    near_from = device(x, 2 * t + zh, y % 2, zh, y)
    far_from = device(x, 2 * t + zh, y % 2, 1 - zh, y)
    greet(far_from)
    near_self = (1 - differ(s, zh)) * even

    @pl.when(near_self == 0)
    def _():
        greet(near_from)

    @pl.when(off > 0)
    def _():
        greet(source)

    listed = st_ref[0, 0] == row
    for k in range(1, 16):
        listed = listed | (st_ref[0, k] == row)
    keep = jnp.where(listed, 1, 0)
    load_m.wait()
    masked = jnp.where(jnp.broadcast_to(keep, (B, B)) > 0, m_in[...], 0.0)
    for q in range(Q):
        m_own[q] = masked[:, q * W:(q + 1) * W]

    pl.semaphore_wait(barrier, 12 + jnp.minimum(off, 1) + even * (4 * apart + 3 * (1 - apart)))

    def remote(src, dst, send, recv, target):
        return pltpu.make_async_remote_copy(
            src_ref=src, dst_ref=dst, send_sem=send, recv_sem=recv,
            device_id=target, device_id_type=MESH,
        )

    sends = []

    def launch(*args):
        copy = remote(*args)
        copy.start()
        sends.append(copy)

    def arrived(buf, recv):
        remote(buf, buf, load_sem.at[0], recv, mate).wait_recv()

    slot_j, slot_i = 2 * s + core, y // 2

    def home_copy(q):
        return remote(m_own.at[q], m_all.at[q, slot_j, slot_i], home_s.at[q], home_r.at[q], home)

    def home_send(q):
        @pl.when(off > 0)
        def _():
            home_copy(q).start()

        @pl.when(off == 0)
        def _():
            pltpu.make_async_copy(m_own.at[q], m_all.at[q, slot_j, slot_i], home_r.at[q]).start()

    def home_left(q):
        @pl.when(off > 0)
        def _():
            home_copy(q).wait_send()

    def next_send(j):
        launch(a_ref.at[:, j * B:(j + 1) * B], a_next.at[j], an_s.at[j], an_r.at[j], nextz)

    def next_pass(j):
        arrived(a_next.at[j], an_r.at[j])
        launch(a_next.at[j], a_far.at[j], af_s.at[j], af_r.at[j], mate)

    home_send(0)
    home_send(1)
    launch(a_ref, a_mate, am_sem.at[0], am_sem.at[1], mate)

    def strip(pair, c):
        return 2 * (s if pair == OWN else 1 - s) + c

    mt_hi[...], mt_lo[...] = split(masked.T)
    load_a.wait()
    a_hi[strip(OWN, core)], a_lo[strip(OWN, core)] = split(a_own[...])

    def z_send(q):
        launch(unit(q, x, t), unit(q, x, t), z_s.at[q], z_r.at[q],
               device(x, (zl + 2) % 4, core, zh, y))

    def x_send(q, a):
        u = unit(q, x, differ(t, a))
        for i, d in enumerate((1, 3)):
            launch(u, u, x_s.at[q, a, i], x_r.at[q, a, i], device((x + d) % 4, zl, core, zh, y))

    def x_arrived(q, a, i):
        arrived(unit(q, x + (3 if i == 0 else 1), differ(t, a)), x_r.at[q, a, i])

    def forward(q):
        for a in range(2):
            x_arrived(q, a, a)
            u = unit(q, x + (3 if a == 0 else 1), differ(t, a))
            launch(u, u, f_s.at[q, a], f_r.at[q, a],
                   device((x + (1 if a == 0 else 3)) % 4, zl, core, zh, y))

    def gathered(q):
        for a in range(2):
            x_arrived(q, a, 1 - a)
        for a in range(2):
            arrived(unit(q, x + 2, differ(t, a)), f_r.at[q, a])
        for j in range(4):
            for i in range(2):
                rows, cols = slice(j * B, (j + 1) * B), slice(i * W, (i + 1) * W)
                m_hi[q, rows, cols], m_lo[q, rows, cols] = split(m_all[q, j, i])

    def home_arrived(q):
        u = unit(q, x, t)
        pltpu.make_async_copy(u, u, home_r.at[q]).wait()

    def multiply(q, pair):
        for c in range(2):
            r = strip(pair, c)
            out = dot3(a_hi[r], a_lo[r], m_hi[q], m_lo[q])
            for i in range(2):
                part[q, r, i] = out[:, i * W:(i + 1) * W]

    over, at_right, at_left, here = ((y + 2) % 4) // 2, right_y // 2, left_y // 2, y // 2

    def first_even(q, pair):
        return (
            remote(part.at[q, strip(pair, 0), over], c1.at[q, pair, 0], e1_s.at[q, pair, 0],
                   c1_r.at[q, pair, 0], right),
            remote(part.at[q, strip(pair, 1), over], c1.at[q, pair, 1], e1_s.at[q, pair, 1],
                   c1_r.at[q, pair, 1], left),
        )

    def to_sum(q, pair, i, c):
        return remote(part.at[q, strip(pair, c), at_right if i == 0 else at_left],
                      c2.at[q, pair, i, c], o_s.at[q, pair, i, c], c2_r.at[q, pair, i, c],
                      right if i == 0 else left)

    def scatter_first(q, pair):
        @pl.when(even == 1)
        def _():
            for copy in first_even(q, pair):
                copy.start()

        @pl.when(even == 0)
        def _():
            to_sum(q, pair, 0, 1).start()
            to_sum(q, pair, 1, 0).start()

    def scatter_second(q, pair):
        @pl.when(even == 0)
        def _():
            for i in range(2):
                arrived(c1.at[q, pair, i], c1_r.at[q, pair, i])
                r, k = strip(pair, i), at_right if i == 0 else at_left
                part[q, r, k] = part[q, r, k] + c1[q, pair, i]
                to_sum(q, pair, i, i).start()

    def to_owner(q, pair, c):
        zl_to = 2 * t + (s if pair == OWN else 1 - s)
        return remote(part.at[q, strip(pair, c), here], nf.at[q, apart], n_s.at[q, pair, c],
                      n_r.at[q, apart], device(x, zl_to, c, s, y))

    def is_self(pair, c):
        if pair == NEXT:
            return None
        return (1 - apart) * (1 - differ(core, c))

    def scatter_last(q, pair):
        @pl.when(even == 1)
        def _():
            for c in range(2):
                for i in range(2):
                    arrived(c2.at[q, pair, i, c], c2_r.at[q, pair, i, c])
                r = strip(pair, c)
                part[q, r, here] = part[q, r, here] + (c2[q, pair, 0, c] + c2[q, pair, 1, c])
                local = is_self(pair, c)
                if local is None:
                    to_owner(q, pair, c).start()
                else:
                    @pl.when(local == 0)
                    def _():
                        to_owner(q, pair, c).start()

                    @pl.when(local == 1)
                    def _():
                        pltpu.make_async_copy(
                            part.at[q, r, here], nf.at[q, 0], n_r.at[q, 0]
                        ).start()

    def slice_copy(q, d):
        e = (me + d) % 8
        return remote(t_buf.at[q, e], t_in.at[q, me], ds_s.at[q, d], ds_r.at[q], peer_x(e))

    def sum_copy(q, d):
        return remote(z_in.at[q, zl], z_in.at[q, zl], dz_s.at[q, d], dz_r.at[q],
                      device(x, (zl + d) % 4, core, zh, y))

    def result_copy(q, d):
        return remote(t_out.at[q, me], t_out.at[q, me], dg_s.at[q, d], dg_r.at[q],
                      peer_x((me + d) % 8))

    def finish(q):
        for i in range(2):
            pltpu.make_async_copy(nf.at[q, i], nf.at[q, i], n_r.at[q, i]).wait()
        total = nf[q, 0] + nf[q, 1]
        panel = jnp.where(jnp.broadcast_to(keep, (B, W)) > 0, -total, 0.0)
        p_ref[:, q * W:(q + 1) * W] = panel
        p_hi, p_lo = split(panel)
        t_buf[q] = dot3(mt_hi[...], mt_lo[...], p_hi, p_lo).reshape(8, 32, W)
        for d in range(1, 8):
            slice_copy(q, d).start()
        t_in[q, me] = t_buf[q, me]

    def diagonal_sum(q):
        arrived(t_in.at[q, pl.ds(0, 7)], ds_r.at[q])
        z_in[q, zl] = jnp.sum(t_in[q], axis=0)
        for d in range(1, 4):
            sum_copy(q, d).start()

    def diagonal_share(q):
        arrived(z_in.at[q, pl.ds(0, 3)], dz_r.at[q])
        first = pl.multiple_of(me * 32, 32)
        t_out[q, me] = dinv[pl.ds(first, 32), q * W:(q + 1) * W] - jnp.sum(z_in[q], axis=0)
        for d in range(1, 8):
            result_copy(q, d).start()

    def diagonal_store(q):
        arrived(t_out.at[q, pl.ds(0, 7)], dg_r.at[q])
        d_ref[:, q * W:(q + 1) * W] = t_out[q].reshape(B, W)

    next_send(0)
    home_arrived(0)
    z_send(0)
    x_send(0, 0)
    next_send(1)
    home_left(0)
    home_left(1)
    arrived(unit(0, x, 1 - t), z_r.at[0])
    x_send(0, 1)
    next_send(2)
    arrived(a_mate, am_sem.at[1])
    a_hi[strip(OWN, 1 - core)], a_lo[strip(OWN, 1 - core)] = split(a_mate[...])
    home_arrived(1)
    z_send(1)
    x_send(1, 0)
    next_send(3)
    forward(0)
    arrived(unit(1, x, 1 - t), z_r.at[1])
    x_send(1, 1)
    next_pass(0)
    next_pass(1)
    gathered(0)
    multiply(0, OWN)
    scatter_first(0, OWN)
    forward(1)
    next_pass(2)
    scatter_second(0, OWN)
    next_pass(3)
    for j in range(4):
        cols = slice(j * B, (j + 1) * B)
        r = strip(NEXT, core)
        a_hi[r, :, cols], a_lo[r, :, cols] = split(a_next[j])
        arrived(a_far.at[j], af_r.at[j])
        r = strip(NEXT, 1 - core)
        a_hi[r, :, cols], a_lo[r, :, cols] = split(a_far[j])
    multiply(0, NEXT)
    scatter_first(0, NEXT)
    scatter_last(0, OWN)
    gathered(1)
    multiply(1, OWN)
    scatter_first(1, OWN)
    scatter_second(0, NEXT)
    multiply(1, NEXT)
    scatter_first(1, NEXT)
    scatter_second(1, OWN)
    scatter_last(0, NEXT)
    scatter_second(1, NEXT)
    load_d.wait()
    scatter_last(1, OWN)
    finish(0)
    scatter_last(1, NEXT)
    diagonal_sum(0)
    finish(1)
    diagonal_share(0)
    diagonal_sum(1)
    diagonal_store(0)
    for copy in sends:
        copy.wait_send()
    for q in range(Q):
        @pl.when(even == 1)
        def _(q=q):
            for pair in range(2):
                for copy in first_even(q, pair):
                    copy.wait_send()
                for c in range(2):
                    local = is_self(pair, c)
                    if local is None:
                        to_owner(q, pair, c).wait_send()
                    else:
                        @pl.when(local == 0)
                        def _():
                            to_owner(q, pair, c).wait_send()

        @pl.when(even == 0)
        def _(q=q):
            for pair in range(2):
                for i in range(2):
                    for c in range(2):
                        to_sum(q, pair, i, c).wait_send()

    def diagonal_left(q):
        for d in range(1, 8):
            slice_copy(q, d).wait_send()
        for d in range(1, 4):
            sum_copy(q, d).wait_send()

    def shared(q):
        for d in range(1, 8):
            result_copy(q, d).wait_send()

    diagonal_share(1)
    diagonal_left(0)
    diagonal_left(1)
    shared(0)
    diagonal_store(1)
    shared(1)


def local(inverse_anc, lower_panel, structure, diag_inverse):
    f32, bf16 = jnp.float32, jnp.bfloat16
    dma = pltpu.SemaphoreType.DMA
    hbm = pl.BlockSpec(memory_space=pl.ANY)
    vmem = pl.BlockSpec(memory_space=pltpu.VMEM)
    return pl.pallas_call(
        kernel,
        out_shape=(jax.ShapeDtypeStruct((B, B), f32), jax.ShapeDtypeStruct((B, B), f32)),
        in_specs=[hbm, hbm, pl.BlockSpec(memory_space=pltpu.SMEM), hbm],
        out_specs=(vmem, vmem),
        scratch_shapes=[
            pltpu.VMEM((B, 4 * B), f32), pltpu.VMEM((B, 4 * B), f32),
            pltpu.VMEM((4, B, B), f32), pltpu.VMEM((4, B, B), f32),
            pltpu.VMEM((4, B, 4 * B), bf16), pltpu.VMEM((4, B, 4 * B), bf16),
            pltpu.VMEM((B, B), f32), pltpu.VMEM((Q, B, W), f32),
            pltpu.VMEM((B, B), bf16), pltpu.VMEM((B, B), bf16),
            pltpu.VMEM((Q, 4, 2, B, W), f32),
            pltpu.VMEM((Q, 4 * B, 2 * W), bf16), pltpu.VMEM((Q, 4 * B, 2 * W), bf16),
            pltpu.VMEM((Q, 4, 2, B, W), f32),
            pltpu.VMEM((Q, 2, 2, B, W), f32), pltpu.VMEM((Q, 2, 2, 2, B, W), f32),
            pltpu.VMEM((Q, 2, B, W), f32),
            pltpu.VMEM((Q, 8, 32, W), f32), pltpu.VMEM((Q, 8, 32, W), f32),
            pltpu.VMEM((Q, 4, 32, W), f32), pltpu.VMEM((Q, 8, 32, W), f32),
            pltpu.VMEM((B, B), f32),
            dma((3,)), dma((2,)), dma((4,)), dma((4,)), dma((4,)), dma((4,)),
            dma((Q,)), dma((Q,)), dma((Q,)), dma((Q,)),
            dma((Q, 2, 2)), dma((Q, 2, 2)), dma((Q, 2)), dma((Q, 2)),
            dma((Q, 2, 2)), dma((Q, 2, 2)), dma((Q, 2, 2, 2)), dma((Q, 2, 2, 2)),
            dma((Q, 2, 2)), dma((Q, 2)),
            dma((Q, 8)), dma((Q,)), dma((Q, 4)), dma((Q,)), dma((Q, 8)), dma((Q,)),
        ],
        compiler_params=pltpu.CompilerParams(
            collective_id=0, has_side_effects=True, vmem_limit_bytes=62 * 2**20
        ),
    )(inverse_anc, lower_panel, structure, diag_inverse)


def solution(mesh):
    placed = (P("row", "col"), P("row", "col"), P("col", None), P("col", None))
    return jax.shard_map(
        local,
        mesh=mesh,
        in_specs=placed,
        out_specs=(P("row", "col"), P("col", None)),
        check_vma=False,
    )
```

```python
import functools

import jax
import jax.numpy as jnp
from jax import lax
from jax.experimental import pallas as pl
from jax.experimental.pallas import tpu as pltpu
from jax.sharding import PartitionSpec as P

MESH = pl.DeviceIdType.MESH
Q = 2
W = 128
B = 256
OWN, NEXT = 0, 1


def device(x, zl, core, zh, y):
    return ((x * 4 + zl) * 2 + core, zh * 4 + y)


def differ(a, b):
    return a + b - 2 * a * b


def split(value):
    high = value.astype(jnp.bfloat16)
    return high, (value - high.astype(jnp.float32)).astype(jnp.bfloat16)


def dot3(a_high, a_low, b_high, b_low):
    dot = functools.partial(jnp.dot, preferred_element_type=jnp.float32)
    return dot(a_high, b_high) + (dot(a_high, b_low) + dot(a_low, b_high))


def kernel(
    a_ref, m_ref, st_ref, dinv_ref, p_ref, d_ref,
    a_own, a_mate, a_next, a_far, a_hi, a_lo, m_in, m_own, mt_hi, mt_lo, m_all, m_hi, m_lo,
    part, c1, c2, nf, t_buf, t_in, z_in, t_out, dinv,
    load_sem, am_sem, an_s, an_r, af_s, af_r, home_s, home_r, z_s, z_r, x_s, x_r, f_s, f_r,
    e1_s, c1_r, o_s, c2_r, n_s, n_r, ds_s, ds_r, dz_s, dz_r, dg_s, dg_r,
):
    row = lax.axis_index("row")
    col = lax.axis_index("col")
    x, zl, core = row // 8, (row // 2) % 4, row % 2
    zh, y = col // 4, col % 4
    t, s = zl // 2, zl % 2

    load_m = pltpu.make_async_copy(m_ref, m_in, load_sem.at[0])
    load_m.start()
    load_a = pltpu.make_async_copy(a_ref, a_own, load_sem.at[1])
    load_a.start()
    load_d = pltpu.make_async_copy(dinv_ref, dinv, load_sem.at[2])
    load_d.start()

    to_zh, to_y = x // 2, (x % 2) * 2 + t
    turn = differ(zh, to_zh) * differ(t, zh)
    to_x = (2 * core + y // 2 + x) % 4
    to_zl = 2 * differ(s, turn) + zh
    home = device(to_x, to_zl, y % 2, to_zh, to_y)
    off = (
        (to_x - x) * (to_x - x) + (to_zl - zl) * (to_zl - zl) + (y % 2 - core) * (y % 2 - core)
        + (to_zh - zh) * (to_zh - zh) + (to_y - y) * (to_y - y)
    )
    from_x = 2 * zh + y // 2
    turned = differ(s, zh) * differ(y % 2, s)

    def block_of(at_x, at_t):
        m = (at_x - from_x + 8) % 4
        return 2 * differ(at_t, turned) + m // 2, m % 2

    def unit(q, at_x, at_t):
        j, i = block_of(at_x, at_t)
        return m_all.at[q, j, i]

    j_here, i_here = block_of(x, t)
    source = device(from_x, 2 * (y % 2) + j_here // 2, j_here % 2, s, 2 * i_here + core)

    even = 1 - differ(core, y % 2)
    apart = differ(zh, s)
    right_y, left_y = (y + 1) % 4, (y + 3) % 4
    right, left = (row, zh * 4 + right_y), (row, zh * 4 + left_y)
    mate = device(x, zl, 1 - core, zh, y)
    nextz = device(x, 2 * t + 1 - s, core, zh, y)
    me = x * 2 + core

    barrier = pltpu.get_barrier_semaphore()

    def greet(target):
        pl.semaphore_signal(barrier, inc=1, device_id=target, device_id_type=MESH)

    def peer_x(e):
        return device(e // 2, zl, e % 2, zh, y)

    for d in range(1, 8):
        greet(peer_x((me + d) % 8))
    for d in range(1, 4):
        greet(device(x, (zl + d) % 4, core, zh, y))
    greet(right)
    greet(left)
    near_from = device(x, 2 * t + zh, y % 2, zh, y)
    far_from = device(x, 2 * t + zh, y % 2, 1 - zh, y)
    greet(far_from)
    near_self = (1 - differ(s, zh)) * even

    @pl.when(near_self == 0)
    def _():
        greet(near_from)

    @pl.when(off > 0)
    def _():
        greet(source)

    listed = st_ref[0, 0] == row
    for k in range(1, 16):
        listed = listed | (st_ref[0, k] == row)
    keep = jnp.where(listed, 1, 0)
    load_m.wait()
    masked = jnp.where(jnp.broadcast_to(keep, (B, B)) > 0, m_in[...], 0.0)
    for q in range(Q):
        m_own[q] = masked[:, q * W:(q + 1) * W]

    pl.semaphore_wait(barrier, 12 + jnp.minimum(off, 1) + even * (4 * apart + 3 * (1 - apart)))

    def remote(src, dst, send, recv, target):
        return pltpu.make_async_remote_copy(
            src_ref=src, dst_ref=dst, send_sem=send, recv_sem=recv,
            device_id=target, device_id_type=MESH,
        )

    sends = []

    def launch(*args):
        copy = remote(*args)
        copy.start()
        sends.append(copy)

    def arrived(buf, recv):
        remote(buf, buf, load_sem.at[0], recv, mate).wait_recv()

    slot_j, slot_i = 2 * s + core, y // 2

    def home_copy(q):
        return remote(m_own.at[q], m_all.at[q, slot_j, slot_i], home_s.at[q], home_r.at[q], home)

    def home_send(q):
        @pl.when(off > 0)
        def _():
            home_copy(q).start()

        @pl.when(off == 0)
        def _():
            pltpu.make_async_copy(m_own.at[q], m_all.at[q, slot_j, slot_i], home_r.at[q]).start()

    def home_left(q):
        @pl.when(off > 0)
        def _():
            home_copy(q).wait_send()

    def next_send(j):
        launch(a_ref.at[:, j * B:(j + 1) * B], a_next.at[j], an_s.at[j], an_r.at[j], nextz)

    def next_pass(j):
        arrived(a_next.at[j], an_r.at[j])
        launch(a_next.at[j], a_far.at[j], af_s.at[j], af_r.at[j], mate)

    home_send(0)
    home_send(1)
    launch(a_ref, a_mate, am_sem.at[0], am_sem.at[1], mate)

    def strip(pair, c):
        return 2 * (s if pair == OWN else 1 - s) + c

    mt_hi[...], mt_lo[...] = split(masked.T)
    load_a.wait()
    a_hi[strip(OWN, core)], a_lo[strip(OWN, core)] = split(a_own[...])

    def z_send(q):
        launch(unit(q, x, t), unit(q, x, t), z_s.at[q], z_r.at[q],
               device(x, (zl + 2) % 4, core, zh, y))

    def x_send(q, a):
        u = unit(q, x, differ(t, a))
        for i, d in enumerate((1, 3)):
            launch(u, u, x_s.at[q, a, i], x_r.at[q, a, i], device((x + d) % 4, zl, core, zh, y))

    def x_arrived(q, a, i):
        arrived(unit(q, x + (3 if i == 0 else 1), differ(t, a)), x_r.at[q, a, i])

    def forward(q):
        for a in range(2):
            x_arrived(q, a, a)
            u = unit(q, x + (3 if a == 0 else 1), differ(t, a))
            launch(u, u, f_s.at[q, a], f_r.at[q, a],
                   device((x + (1 if a == 0 else 3)) % 4, zl, core, zh, y))

    def gathered(q):
        for a in range(2):
            x_arrived(q, a, 1 - a)
        for a in range(2):
            arrived(unit(q, x + 2, differ(t, a)), f_r.at[q, a])
        for j in range(4):
            for i in range(2):
                rows, cols = slice(j * B, (j + 1) * B), slice(i * W, (i + 1) * W)
                m_hi[q, rows, cols], m_lo[q, rows, cols] = split(m_all[q, j, i])

    def home_arrived(q):
        u = unit(q, x, t)
        pltpu.make_async_copy(u, u, home_r.at[q]).wait()

    def multiply(q, pair):
        for c in range(2):
            r = strip(pair, c)
            out = dot3(a_hi[r], a_lo[r], m_hi[q], m_lo[q])
            for i in range(2):
                part[q, r, i] = out[:, i * W:(i + 1) * W]

    over, at_right, at_left, here = ((y + 2) % 4) // 2, right_y // 2, left_y // 2, y // 2

    def first_even(q, pair):
        return (
            remote(part.at[q, strip(pair, 0), over], c1.at[q, pair, 0], e1_s.at[q, pair, 0],
                   c1_r.at[q, pair, 0], right),
            remote(part.at[q, strip(pair, 1), over], c1.at[q, pair, 1], e1_s.at[q, pair, 1],
                   c1_r.at[q, pair, 1], left),
        )

    def to_sum(q, pair, i, c):
        return remote(part.at[q, strip(pair, c), at_right if i == 0 else at_left],
                      c2.at[q, pair, i, c], o_s.at[q, pair, i, c], c2_r.at[q, pair, i, c],
                      right if i == 0 else left)

    def scatter_first(q, pair):
        @pl.when(even == 1)
        def _():
            for copy in first_even(q, pair):
                copy.start()

        @pl.when(even == 0)
        def _():
            to_sum(q, pair, 0, 1).start()
            to_sum(q, pair, 1, 0).start()

    def scatter_second(q, pair):
        @pl.when(even == 0)
        def _():
            for i in range(2):
                arrived(c1.at[q, pair, i], c1_r.at[q, pair, i])
                r, k = strip(pair, i), at_right if i == 0 else at_left
                part[q, r, k] = part[q, r, k] + c1[q, pair, i]
                to_sum(q, pair, i, i).start()

    def to_owner(q, pair, c):
        zl_to = 2 * t + (s if pair == OWN else 1 - s)
        return remote(part.at[q, strip(pair, c), here], nf.at[q, apart], n_s.at[q, pair, c],
                      n_r.at[q, apart], device(x, zl_to, c, s, y))

    def is_self(pair, c):
        if pair == NEXT:
            return None
        return (1 - apart) * (1 - differ(core, c))

    def scatter_last(q, pair):
        @pl.when(even == 1)
        def _():
            for c in range(2):
                for i in range(2):
                    arrived(c2.at[q, pair, i, c], c2_r.at[q, pair, i, c])
                r = strip(pair, c)
                part[q, r, here] = part[q, r, here] + (c2[q, pair, 0, c] + c2[q, pair, 1, c])
                local = is_self(pair, c)
                if local is None:
                    to_owner(q, pair, c).start()
                else:
                    @pl.when(local == 0)
                    def _():
                        to_owner(q, pair, c).start()

                    @pl.when(local == 1)
                    def _():
                        pltpu.make_async_copy(
                            part.at[q, r, here], nf.at[q, 0], n_r.at[q, 0]
                        ).start()

    def slice_copy(q, d):
        e = (me + d) % 8
        return remote(t_buf.at[q, e], t_in.at[q, me], ds_s.at[q, d], ds_r.at[q], peer_x(e))

    def sum_copy(q, d):
        return remote(z_in.at[q, zl], z_in.at[q, zl], dz_s.at[q, d], dz_r.at[q],
                      device(x, (zl + d) % 4, core, zh, y))

    def result_copy(q, d):
        return remote(t_out.at[q, me], t_out.at[q, me], dg_s.at[q, d], dg_r.at[q],
                      peer_x((me + d) % 8))

    def finish(q):
        for i in range(2):
            pltpu.make_async_copy(nf.at[q, i], nf.at[q, i], n_r.at[q, i]).wait()
        total = nf[q, 0] + nf[q, 1]
        panel = jnp.where(jnp.broadcast_to(keep, (B, W)) > 0, -total, 0.0)
        p_ref[:, q * W:(q + 1) * W] = panel
        p_hi, p_lo = split(panel)
        t_buf[q] = dot3(mt_hi[...], mt_lo[...], p_hi, p_lo).reshape(8, 32, W)
        for d in range(1, 8):
            slice_copy(q, d).start()
        t_in[q, me] = t_buf[q, me]

    def diagonal_sum(q):
        arrived(t_in.at[q, pl.ds(0, 7)], ds_r.at[q])
        z_in[q, zl] = jnp.sum(t_in[q], axis=0)
        for d in range(1, 4):
            sum_copy(q, d).start()

    def diagonal_share(q):
        arrived(z_in.at[q, pl.ds(0, 3)], dz_r.at[q])
        first = pl.multiple_of(me * 32, 32)
        t_out[q, me] = dinv[pl.ds(first, 32), q * W:(q + 1) * W] - jnp.sum(z_in[q], axis=0)
        for d in range(1, 8):
            result_copy(q, d).start()

    def diagonal_store(q):
        arrived(t_out.at[q, pl.ds(0, 7)], dg_r.at[q])
        d_ref[:, q * W:(q + 1) * W] = t_out[q].reshape(B, W)

    next_send(0)
    home_arrived(0)
    z_send(0)
    x_send(0, 0)
    next_send(1)
    home_left(0)
    home_left(1)
    arrived(unit(0, x, 1 - t), z_r.at[0])
    x_send(0, 1)
    next_send(2)
    home_arrived(1)
    z_send(1)
    x_send(1, 0)
    next_send(3)
    forward(0)
    arrived(unit(1, x, 1 - t), z_r.at[1])
    x_send(1, 1)
    arrived(a_mate, am_sem.at[1])
    a_hi[strip(OWN, 1 - core)], a_lo[strip(OWN, 1 - core)] = split(a_mate[...])
    next_pass(0)
    next_pass(1)
    gathered(0)
    multiply(0, OWN)
    scatter_first(0, OWN)
    forward(1)
    next_pass(2)
    scatter_second(0, OWN)
    next_pass(3)
    for j in range(4):
        cols = slice(j * B, (j + 1) * B)
        r = strip(NEXT, core)
        a_hi[r, :, cols], a_lo[r, :, cols] = split(a_next[j])
        arrived(a_far.at[j], af_r.at[j])
        r = strip(NEXT, 1 - core)
        a_hi[r, :, cols], a_lo[r, :, cols] = split(a_far[j])
    multiply(0, NEXT)
    scatter_first(0, NEXT)
    scatter_last(0, OWN)
    gathered(1)
    multiply(1, OWN)
    scatter_first(1, OWN)
    scatter_second(0, NEXT)
    multiply(1, NEXT)
    scatter_first(1, NEXT)
    scatter_second(1, OWN)
    scatter_last(0, NEXT)
    scatter_second(1, NEXT)
    load_d.wait()
    scatter_last(1, OWN)
    scatter_last(1, NEXT)
    finish(0)
    diagonal_sum(0)
    finish(1)
    diagonal_share(0)
    diagonal_sum(1)
    diagonal_store(0)
    for copy in sends:
        copy.wait_send()
    for q in range(Q):
        @pl.when(even == 1)
        def _(q=q):
            for pair in range(2):
                for copy in first_even(q, pair):
                    copy.wait_send()
                for c in range(2):
                    local = is_self(pair, c)
                    if local is None:
                        to_owner(q, pair, c).wait_send()
                    else:
                        @pl.when(local == 0)
                        def _():
                            to_owner(q, pair, c).wait_send()

        @pl.when(even == 0)
        def _(q=q):
            for pair in range(2):
                for i in range(2):
                    for c in range(2):
                        to_sum(q, pair, i, c).wait_send()

    def diagonal_left(q):
        for d in range(1, 8):
            slice_copy(q, d).wait_send()
        for d in range(1, 4):
            sum_copy(q, d).wait_send()

    def shared(q):
        for d in range(1, 8):
            result_copy(q, d).wait_send()

    diagonal_share(1)
    diagonal_left(0)
    diagonal_left(1)
    shared(0)
    diagonal_store(1)
    shared(1)


def local(inverse_anc, lower_panel, structure, diag_inverse):
    f32, bf16 = jnp.float32, jnp.bfloat16
    dma = pltpu.SemaphoreType.DMA
    hbm = pl.BlockSpec(memory_space=pl.ANY)
    vmem = pl.BlockSpec(memory_space=pltpu.VMEM)
    return pl.pallas_call(
        kernel,
        out_shape=(jax.ShapeDtypeStruct((B, B), f32), jax.ShapeDtypeStruct((B, B), f32)),
        in_specs=[hbm, hbm, pl.BlockSpec(memory_space=pltpu.SMEM), hbm],
        out_specs=(vmem, vmem),
        scratch_shapes=[
            pltpu.VMEM((B, 4 * B), f32), pltpu.VMEM((B, 4 * B), f32),
            pltpu.VMEM((4, B, B), f32), pltpu.VMEM((4, B, B), f32),
            pltpu.VMEM((4, B, 4 * B), bf16), pltpu.VMEM((4, B, 4 * B), bf16),
            pltpu.VMEM((B, B), f32), pltpu.VMEM((Q, B, W), f32),
            pltpu.VMEM((B, B), bf16), pltpu.VMEM((B, B), bf16),
            pltpu.VMEM((Q, 4, 2, B, W), f32),
            pltpu.VMEM((Q, 4 * B, 2 * W), bf16), pltpu.VMEM((Q, 4 * B, 2 * W), bf16),
            pltpu.VMEM((Q, 4, 2, B, W), f32),
            pltpu.VMEM((Q, 2, 2, B, W), f32), pltpu.VMEM((Q, 2, 2, 2, B, W), f32),
            pltpu.VMEM((Q, 2, B, W), f32),
            pltpu.VMEM((Q, 8, 32, W), f32), pltpu.VMEM((Q, 8, 32, W), f32),
            pltpu.VMEM((Q, 4, 32, W), f32), pltpu.VMEM((Q, 8, 32, W), f32),
            pltpu.VMEM((B, B), f32),
            dma((3,)), dma((2,)), dma((4,)), dma((4,)), dma((4,)), dma((4,)),
            dma((Q,)), dma((Q,)), dma((Q,)), dma((Q,)),
            dma((Q, 2, 2)), dma((Q, 2, 2)), dma((Q, 2)), dma((Q, 2)),
            dma((Q, 2, 2)), dma((Q, 2, 2)), dma((Q, 2, 2, 2)), dma((Q, 2, 2, 2)),
            dma((Q, 2, 2)), dma((Q, 2)),
            dma((Q, 8)), dma((Q,)), dma((Q, 4)), dma((Q,)), dma((Q, 8)), dma((Q,)),
        ],
        compiler_params=pltpu.CompilerParams(
            collective_id=0, has_side_effects=True, vmem_limit_bytes=62 * 2**20
        ),
    )(inverse_anc, lower_panel, structure, diag_inverse)


def solution(mesh):
    placed = (P("row", "col"), P("row", "col"), P("col", None), P("col", None))
    return jax.shard_map(
        local,
        mesh=mesh,
        in_specs=placed,
        out_specs=(P("row", "col"), P("col", None)),
        check_vma=False,
    )
```

```python
import functools

import jax
import jax.numpy as jnp
from jax import lax
from jax.experimental import pallas as pl
from jax.experimental.pallas import tpu as pltpu
from jax.sharding import PartitionSpec as P

MESH = pl.DeviceIdType.MESH
Q = 2
W = 128
B = 256
OWN, NEXT = 0, 1


def device(x, zl, core, zh, y):
    return ((x * 4 + zl) * 2 + core, zh * 4 + y)


def differ(a, b):
    return a + b - 2 * a * b


def split(value):
    high = value.astype(jnp.bfloat16)
    return high, (value - high.astype(jnp.float32)).astype(jnp.bfloat16)


def dot3(a_high, a_low, b_high, b_low):
    dot = functools.partial(jnp.dot, preferred_element_type=jnp.float32)
    return dot(a_high, b_high) + (dot(a_high, b_low) + dot(a_low, b_high))


def kernel(
    a_ref, m_ref, st_ref, dinv_ref, p_ref, d_ref,
    a_own, a_mate, a_next, a_far, a_hi, a_lo, m_in, m_own, mt_hi, mt_lo, m_all, m_hi, m_lo,
    part, c1, c2, nf, t_buf, t_in, z_in, t_out, dinv,
    load_sem, am_sem, an_s, an_r, af_s, af_r, home_s, home_r, z_s, z_r, x_s, x_r, f_s, f_r,
    e1_s, c1_r, o_s, c2_r, n_s, n_r, ds_s, ds_r, dz_s, dz_r, dg_s, dg_r,
):
    row = lax.axis_index("row")
    col = lax.axis_index("col")
    x, zl, core = row // 8, (row // 2) % 4, row % 2
    zh, y = col // 4, col % 4
    t, s = zl // 2, zl % 2

    load_m = pltpu.make_async_copy(m_ref, m_in, load_sem.at[0])
    load_m.start()
    load_a = pltpu.make_async_copy(a_ref, a_own, load_sem.at[1])
    load_a.start()
    load_d = pltpu.make_async_copy(dinv_ref, dinv, load_sem.at[2])
    load_d.start()

    to_zh, to_y = x // 2, (x % 2) * 2 + t
    turn = differ(zh, to_zh) * differ(t, zh)
    to_x = (2 * core + y // 2 + x) % 4
    to_zl = 2 * differ(s, turn) + zh
    home = device(to_x, to_zl, y % 2, to_zh, to_y)
    off = (
        (to_x - x) * (to_x - x) + (to_zl - zl) * (to_zl - zl) + (y % 2 - core) * (y % 2 - core)
        + (to_zh - zh) * (to_zh - zh) + (to_y - y) * (to_y - y)
    )
    from_x = 2 * zh + y // 2
    turned = differ(s, zh) * differ(y % 2, s)

    def block_of(at_x, at_t):
        m = (at_x - from_x + 8) % 4
        return 2 * differ(at_t, turned) + m // 2, m % 2

    def unit(q, at_x, at_t):
        j, i = block_of(at_x, at_t)
        return m_all.at[q, j, i]

    j_here, i_here = block_of(x, t)
    source = device(from_x, 2 * (y % 2) + j_here // 2, j_here % 2, s, 2 * i_here + core)

    even = 1 - differ(core, y % 2)
    apart = differ(zh, s)
    right_y, left_y = (y + 1) % 4, (y + 3) % 4
    right, left = (row, zh * 4 + right_y), (row, zh * 4 + left_y)
    mate = device(x, zl, 1 - core, zh, y)
    nextz = device(x, 2 * t + 1 - s, core, zh, y)
    me = x * 2 + core

    barrier = pltpu.get_barrier_semaphore()

    def greet(target):
        pl.semaphore_signal(barrier, inc=1, device_id=target, device_id_type=MESH)

    def peer_x(e):
        return device(e // 2, zl, e % 2, zh, y)

    for d in range(1, 8):
        greet(peer_x((me + d) % 8))
    for d in range(1, 4):
        greet(device(x, (zl + d) % 4, core, zh, y))
    greet(right)
    greet(left)
    near_from = device(x, 2 * t + zh, y % 2, zh, y)
    far_from = device(x, 2 * t + zh, y % 2, 1 - zh, y)
    greet(far_from)
    near_self = (1 - differ(s, zh)) * even

    @pl.when(near_self == 0)
    def _():
        greet(near_from)

    @pl.when(off > 0)
    def _():
        greet(source)

    listed = st_ref[0, 0] == row
    for k in range(1, 16):
        listed = listed | (st_ref[0, k] == row)
    keep = jnp.where(listed, 1, 0)
    load_m.wait()
    masked = jnp.where(jnp.broadcast_to(keep, (B, B)) > 0, m_in[...], 0.0)
    for q in range(Q):
        m_own[q] = masked[:, q * W:(q + 1) * W]

    pl.semaphore_wait(barrier, 12 + jnp.minimum(off, 1) + even * (4 * apart + 3 * (1 - apart)))

    def remote(src, dst, send, recv, target):
        return pltpu.make_async_remote_copy(
            src_ref=src, dst_ref=dst, send_sem=send, recv_sem=recv,
            device_id=target, device_id_type=MESH,
        )

    sends = []

    def launch(*args):
        copy = remote(*args)
        copy.start()
        sends.append(copy)

    def arrived(buf, recv):
        remote(buf, buf, load_sem.at[0], recv, mate).wait_recv()

    slot_j, slot_i = 2 * s + core, y // 2

    def home_copy(q):
        return remote(m_own.at[q], m_all.at[q, slot_j, slot_i], home_s.at[q], home_r.at[q], home)

    def home_send(q):
        @pl.when(off > 0)
        def _():
            home_copy(q).start()

        @pl.when(off == 0)
        def _():
            pltpu.make_async_copy(m_own.at[q], m_all.at[q, slot_j, slot_i], home_r.at[q]).start()

    def home_left(q):
        @pl.when(off > 0)
        def _():
            home_copy(q).wait_send()

    def next_send(j):
        launch(a_ref.at[:, j * B:(j + 1) * B], a_next.at[j], an_s.at[j], an_r.at[j], nextz)

    def next_pass(j):
        arrived(a_next.at[j], an_r.at[j])
        launch(a_next.at[j], a_far.at[j], af_s.at[j], af_r.at[j], mate)

    home_send(0)
    home_send(1)
    launch(a_ref, a_mate, am_sem.at[0], am_sem.at[1], mate)

    def strip(pair, c):
        return 2 * (s if pair == OWN else 1 - s) + c

    mt_hi[...], mt_lo[...] = split(masked.T)
    load_a.wait()
    a_hi[strip(OWN, core)], a_lo[strip(OWN, core)] = split(a_own[...])

    def z_send(q):
        launch(unit(q, x, t), unit(q, x, t), z_s.at[q], z_r.at[q],
               device(x, (zl + 2) % 4, core, zh, y))

    def x_send(q, a):
        u = unit(q, x, differ(t, a))
        for i, d in enumerate((1, 3)):
            launch(u, u, x_s.at[q, a, i], x_r.at[q, a, i], device((x + d) % 4, zl, core, zh, y))

    def x_arrived(q, a, i):
        arrived(unit(q, x + (3 if i == 0 else 1), differ(t, a)), x_r.at[q, a, i])

    def forward(q):
        for a in range(2):
            x_arrived(q, a, a)
            u = unit(q, x + (3 if a == 0 else 1), differ(t, a))
            launch(u, u, f_s.at[q, a], f_r.at[q, a],
                   device((x + (1 if a == 0 else 3)) % 4, zl, core, zh, y))

    def gathered(q):
        for a in range(2):
            x_arrived(q, a, 1 - a)
        for a in range(2):
            arrived(unit(q, x + 2, differ(t, a)), f_r.at[q, a])
        for j in range(4):
            for i in range(2):
                rows, cols = slice(j * B, (j + 1) * B), slice(i * W, (i + 1) * W)
                m_hi[q, rows, cols], m_lo[q, rows, cols] = split(m_all[q, j, i])

    def home_arrived(q):
        u = unit(q, x, t)
        pltpu.make_async_copy(u, u, home_r.at[q]).wait()

    def split_next(j):
        cols = slice(j * B, (j + 1) * B)
        r = strip(NEXT, core)
        a_hi[r, :, cols], a_lo[r, :, cols] = split(a_next[j])

    def split_far(j):
        arrived(a_far.at[j], af_r.at[j])
        cols = slice(j * B, (j + 1) * B)
        r = strip(NEXT, 1 - core)
        a_hi[r, :, cols], a_lo[r, :, cols] = split(a_far[j])

    def multiply(q, pair):
        for c in range(2):
            r = strip(pair, c)
            out = dot3(a_hi[r], a_lo[r], m_hi[q], m_lo[q])
            for i in range(2):
                part[q, r, i] = out[:, i * W:(i + 1) * W]

    over, at_right, at_left, here = ((y + 2) % 4) // 2, right_y // 2, left_y // 2, y // 2

    def first_even(q, pair):
        return (
            remote(part.at[q, strip(pair, 0), over], c1.at[q, pair, 0], e1_s.at[q, pair, 0],
                   c1_r.at[q, pair, 0], right),
            remote(part.at[q, strip(pair, 1), over], c1.at[q, pair, 1], e1_s.at[q, pair, 1],
                   c1_r.at[q, pair, 1], left),
        )

    def to_sum(q, pair, i, c):
        return remote(part.at[q, strip(pair, c), at_right if i == 0 else at_left],
                      c2.at[q, pair, i, c], o_s.at[q, pair, i, c], c2_r.at[q, pair, i, c],
                      right if i == 0 else left)

    def scatter_first(q, pair):
        @pl.when(even == 1)
        def _():
            for copy in first_even(q, pair):
                copy.start()

        @pl.when(even == 0)
        def _():
            to_sum(q, pair, 0, 1).start()
            to_sum(q, pair, 1, 0).start()

    def scatter_second(q, pair):
        @pl.when(even == 0)
        def _():
            for i in range(2):
                arrived(c1.at[q, pair, i], c1_r.at[q, pair, i])
                r, k = strip(pair, i), at_right if i == 0 else at_left
                part[q, r, k] = part[q, r, k] + c1[q, pair, i]
                to_sum(q, pair, i, i).start()

    def to_owner(q, pair, c):
        zl_to = 2 * t + (s if pair == OWN else 1 - s)
        return remote(part.at[q, strip(pair, c), here], nf.at[q, apart], n_s.at[q, pair, c],
                      n_r.at[q, apart], device(x, zl_to, c, s, y))

    def is_self(pair, c):
        if pair == NEXT:
            return None
        return (1 - apart) * (1 - differ(core, c))

    def scatter_last(q, pair):
        @pl.when(even == 1)
        def _():
            for c in range(2):
                for i in range(2):
                    arrived(c2.at[q, pair, i, c], c2_r.at[q, pair, i, c])
                r = strip(pair, c)
                part[q, r, here] = part[q, r, here] + (c2[q, pair, 0, c] + c2[q, pair, 1, c])
                local = is_self(pair, c)
                if local is None:
                    to_owner(q, pair, c).start()
                else:
                    @pl.when(local == 0)
                    def _():
                        to_owner(q, pair, c).start()

                    @pl.when(local == 1)
                    def _():
                        pltpu.make_async_copy(
                            part.at[q, r, here], nf.at[q, 0], n_r.at[q, 0]
                        ).start()

    def slice_copy(q, d):
        e = (me + d) % 8
        return remote(t_buf.at[q, e], t_in.at[q, me], ds_s.at[q, d], ds_r.at[q], peer_x(e))

    def sum_copy(q, d):
        return remote(z_in.at[q, zl], z_in.at[q, zl], dz_s.at[q, d], dz_r.at[q],
                      device(x, (zl + d) % 4, core, zh, y))

    def result_copy(q, d):
        return remote(t_out.at[q, me], t_out.at[q, me], dg_s.at[q, d], dg_r.at[q],
                      peer_x((me + d) % 8))

    def finish(q):
        for i in range(2):
            pltpu.make_async_copy(nf.at[q, i], nf.at[q, i], n_r.at[q, i]).wait()
        total = nf[q, 0] + nf[q, 1]
        panel = jnp.where(jnp.broadcast_to(keep, (B, W)) > 0, -total, 0.0)
        p_ref[:, q * W:(q + 1) * W] = panel
        p_hi, p_lo = split(panel)
        t_buf[q] = dot3(mt_hi[...], mt_lo[...], p_hi, p_lo).reshape(8, 32, W)
        for d in (4, 3, 5, 2, 6, 7, 1):
            slice_copy(q, d).start()
        t_in[q, me] = t_buf[q, me]

    def diagonal_sum(q):
        arrived(t_in.at[q, pl.ds(0, 7)], ds_r.at[q])
        z_in[q, zl] = jnp.sum(t_in[q], axis=0)
        for d in range(1, 4):
            sum_copy(q, d).start()

    def diagonal_share(q):
        arrived(z_in.at[q, pl.ds(0, 3)], dz_r.at[q])
        first = pl.multiple_of(me * 32, 32)
        t_out[q, me] = dinv[pl.ds(first, 32), q * W:(q + 1) * W] - jnp.sum(z_in[q], axis=0)
        for d in (4, 3, 5, 2, 6, 7, 1):
            result_copy(q, d).start()

    def diagonal_store(q):
        arrived(t_out.at[q, pl.ds(0, 7)], dg_r.at[q])
        d_ref[:, q * W:(q + 1) * W] = t_out[q].reshape(B, W)

    next_send(0)
    home_arrived(0)
    z_send(0)
    x_send(0, 0)
    next_send(1)
    home_left(0)
    home_left(1)
    arrived(unit(0, x, 1 - t), z_r.at[0])
    x_send(0, 1)
    next_send(2)
    home_arrived(1)
    z_send(1)
    x_send(1, 0)
    next_send(3)
    forward(0)
    arrived(unit(1, x, 1 - t), z_r.at[1])
    x_send(1, 1)
    arrived(a_mate, am_sem.at[1])
    a_hi[strip(OWN, 1 - core)], a_lo[strip(OWN, 1 - core)] = split(a_mate[...])
    next_pass(0)
    next_pass(1)
    gathered(0)
    multiply(0, OWN)
    scatter_first(0, OWN)
    forward(1)
    next_pass(2)
    scatter_second(0, OWN)
    for j in range(3):
        split_next(j)
    split_far(0)
    split_far(1)
    next_pass(3)
    split_far(2)
    split_next(3)
    split_far(3)
    multiply(0, NEXT)
    scatter_first(0, NEXT)
    scatter_last(0, OWN)
    gathered(1)
    multiply(1, OWN)
    scatter_first(1, OWN)
    scatter_second(0, NEXT)
    multiply(1, NEXT)
    scatter_first(1, NEXT)
    scatter_second(1, OWN)
    scatter_last(0, NEXT)
    scatter_second(1, NEXT)
    load_d.wait()
    scatter_last(1, OWN)
    scatter_last(1, NEXT)
    finish(0)
    diagonal_sum(0)
    finish(1)
    diagonal_share(0)
    diagonal_sum(1)
    diagonal_store(0)
    for copy in sends:
        copy.wait_send()
    for q in range(Q):
        @pl.when(even == 1)
        def _(q=q):
            for pair in range(2):
                for copy in first_even(q, pair):
                    copy.wait_send()
                for c in range(2):
                    local = is_self(pair, c)
                    if local is None:
                        to_owner(q, pair, c).wait_send()
                    else:
                        @pl.when(local == 0)
                        def _():
                            to_owner(q, pair, c).wait_send()

        @pl.when(even == 0)
        def _(q=q):
            for pair in range(2):
                for i in range(2):
                    for c in range(2):
                        to_sum(q, pair, i, c).wait_send()

    def diagonal_left(q):
        for d in range(1, 8):
            slice_copy(q, d).wait_send()
        for d in range(1, 4):
            sum_copy(q, d).wait_send()

    def shared(q):
        for d in range(1, 8):
            result_copy(q, d).wait_send()

    diagonal_share(1)
    diagonal_left(0)
    diagonal_left(1)
    shared(0)
    diagonal_store(1)
    shared(1)


def local(inverse_anc, lower_panel, structure, diag_inverse):
    f32, bf16 = jnp.float32, jnp.bfloat16
    dma = pltpu.SemaphoreType.DMA
    hbm = pl.BlockSpec(memory_space=pl.ANY)
    vmem = pl.BlockSpec(memory_space=pltpu.VMEM)
    return pl.pallas_call(
        kernel,
        out_shape=(jax.ShapeDtypeStruct((B, B), f32), jax.ShapeDtypeStruct((B, B), f32)),
        in_specs=[hbm, hbm, pl.BlockSpec(memory_space=pltpu.SMEM), hbm],
        out_specs=(vmem, vmem),
        scratch_shapes=[
            pltpu.VMEM((B, 4 * B), f32), pltpu.VMEM((B, 4 * B), f32),
            pltpu.VMEM((4, B, B), f32), pltpu.VMEM((4, B, B), f32),
            pltpu.VMEM((4, B, 4 * B), bf16), pltpu.VMEM((4, B, 4 * B), bf16),
            pltpu.VMEM((B, B), f32), pltpu.VMEM((Q, B, W), f32),
            pltpu.VMEM((B, B), bf16), pltpu.VMEM((B, B), bf16),
            pltpu.VMEM((Q, 4, 2, B, W), f32),
            pltpu.VMEM((Q, 4 * B, 2 * W), bf16), pltpu.VMEM((Q, 4 * B, 2 * W), bf16),
            pltpu.VMEM((Q, 4, 2, B, W), f32),
            pltpu.VMEM((Q, 2, 2, B, W), f32), pltpu.VMEM((Q, 2, 2, 2, B, W), f32),
            pltpu.VMEM((Q, 2, B, W), f32),
            pltpu.VMEM((Q, 8, 32, W), f32), pltpu.VMEM((Q, 8, 32, W), f32),
            pltpu.VMEM((Q, 4, 32, W), f32), pltpu.VMEM((Q, 8, 32, W), f32),
            pltpu.VMEM((B, B), f32),
            dma((3,)), dma((2,)), dma((4,)), dma((4,)), dma((4,)), dma((4,)),
            dma((Q,)), dma((Q,)), dma((Q,)), dma((Q,)),
            dma((Q, 2, 2)), dma((Q, 2, 2)), dma((Q, 2)), dma((Q, 2)),
            dma((Q, 2, 2)), dma((Q, 2, 2)), dma((Q, 2, 2, 2)), dma((Q, 2, 2, 2)),
            dma((Q, 2, 2)), dma((Q, 2)),
            dma((Q, 8)), dma((Q,)), dma((Q, 4)), dma((Q,)), dma((Q, 8)), dma((Q,)),
        ],
        compiler_params=pltpu.CompilerParams(
            collective_id=0, has_side_effects=True, vmem_limit_bytes=62 * 2**20
        ),
    )(inverse_anc, lower_panel, structure, diag_inverse)


def solution(mesh):
    placed = (P("row", "col"), P("row", "col"), P("col", None), P("col", None))
    return jax.shard_map(
        local,
        mesh=mesh,
        in_specs=placed,
        out_specs=(P("row", "col"), P("col", None)),
        check_vma=False,
    )
```
